256 devices in a mesh: section: 2 (over y_hi), lat: 16 (over x, y_lo, core), lon: 8 (over z).
Axes of the slice: x: 4, y: 4 (y_hi: 2, y_lo: 2; y = y_hi * 2 + y_lo), z: 8, core: 2. Of those that a mesh axis runs over, the one named last changes fastest.
Arguments:
- fields: bfloat16 [128, 1024, 1920], P(('lat', 'lon'), 'section'), may hold values from -6 to 6
- embed_weight: bfloat16 [128, 4, 4, 512], replicated, may hold values from -0.125 to 0.125
- embed_bias: float32 [512], replicated, may hold values from -3 to 3
- conv_weights: bfloat16 [2, 3, 3, 512, 512], replicated, may hold values from -0.09375 to 0.09375
- conv_bias: float32 [2, 512], replicated, may hold values from -3 to 3
Outputs:
- encoded: bfloat16 [256, 480, 512], P(('section', 'lat'), 'lon')
The draws below stay inside these ranges and needn't reach their ends.
All inputs are finite; a program needn't handle non-finite values.
Results may differ from the reference program's by a relative error of at most 0.007.
Values may be sent and summed in bfloat16 or wider, within the bound.
A program may use at most 128 MiB of HBM per device.

```python
import jax
import jax.numpy as jnp
from jax import lax

VARS = 128
WIDTH = 512
PATCH = 4
LAYERS = 2
NROWS = 1024
NCOLS = 1920


def block_levels(key, extent, shards, least, high):
    gain = 1.0
    for position, shards_of in shards:
        steps = jax.random.uniform(jax.random.fold_in(jax.random.fold_in(key, 6), position), (shards_of,), jnp.float32, least / len(shards), high / len(shards))
        gain = gain * jnp.repeat(jnp.exp(steps), extent[position] // shards_of).reshape((-1,) + (1,) * (len(extent) - 1 - position))
    return gain


def normal_values(key, dims, spread, bound, cuts=(), dtype=jnp.bfloat16):
    drawn = spread * jax.random.normal(key, dims, jnp.float32)
    if cuts:
        drawn = drawn * block_levels(key, dims, cuts, -0.22, 0.18)
    return jnp.clip(drawn, -bound, bound).astype(dtype)


def setup_inputs(seed: int = 0) -> dict:
    keys = jax.random.split(jax.random.key(seed), 6)
    return {
        "fields": normal_values(keys[0], (VARS, NROWS, NCOLS), 1.0, 6.0, ((0, 128), (1, 2))),
        "embed_weight": normal_values(keys[1], (VARS, PATCH, PATCH, WIDTH), (VARS * PATCH * PATCH) ** -0.5, 0.125),
        "embed_bias": normal_values(keys[2], (WIDTH,), 0.5, 3.0, (), jnp.float32),
        "conv_weights": normal_values(keys[3], (LAYERS, 3, 3, WIDTH, WIDTH), (9 * WIDTH) ** -0.5, 0.09375),
        "conv_bias": normal_values(keys[4], (LAYERS, WIDTH), 0.5, 3.0, (), jnp.float32),
    }


def normalize(hidden):
    values = hidden.astype(jnp.float32)
    scale = jax.lax.rsqrt(lax.optimization_barrier(jnp.mean(values * values, axis=-1, keepdims=True)) + 1e-06)
    return (values * scale).astype(jnp.bfloat16)

def reference(fields, embed_weight, embed_bias, conv_weights, conv_bias):
    vars_count, rows, cols = fields.shape
    patches = fields.reshape(vars_count, rows // PATCH, PATCH, cols // PATCH, PATCH).astype(jnp.float32)
    tokens = jnp.einsum('vakbl,vklc->abc', patches, embed_weight.astype(jnp.float32)) + embed_bias
    hidden = tokens.astype(jnp.bfloat16)
    prow, pcol = (rows // PATCH, cols // PATCH)
    for layer in range(LAYERS):
        normed = normalize(hidden)
        wrapped = jnp.concatenate([normed[:, -1:], normed, normed[:, :1]], axis=1)
        padded = jnp.pad(wrapped, ((1, 1), (0, 0), (0, 0)))
        conv = jnp.zeros((prow * pcol, WIDTH), jnp.float32) + conv_bias[layer]
        for i in range(3):
            for j in range(3):
                window = padded[i:i + prow, j:j + pcol].reshape(prow * pcol, WIDTH)
                conv = conv + jnp.dot(window, conv_weights[layer, i, j], preferred_element_type=jnp.float32)
        conv = conv.reshape(prow, pcol, WIDTH)
        hidden = (hidden.astype(jnp.float32) + jax.nn.gelu(conv)).astype(jnp.bfloat16)
    return hidden
```

```python
import jax
import jax.numpy as jnp
from jax import lax
from jax.experimental import pallas as pl
from jax.experimental.pallas import tpu as pltpu
from jax.sharding import PartitionSpec as P

MESH = pl.DeviceIdType.MESH
F32 = jnp.float32
BF16 = jnp.bfloat16

LAT = 16
LON = 8
PATCH = 4
ROWS = 8
COLS = 60
WIDTH = 512
PITCH = 64
TOKENS = ROWS * PITCH
CELL_COLS = COLS * PATCH
CELL_ROWS = ROWS * PATCH
WINDOW = 384
LAST_START = 1920 - WINDOW
MAX_SHIFT = 144
CHUNKS = 4
CHUNK = TOKENS // CHUNKS
ORDER = (0, 3, 1, 2)
PADDED = (ROWS + 4) * PITCH
BLOCK = 16 * 16
EPS = 1e-06


def kernel(
    fields, embed_w, embed_b, conv_w, conv_b, out,
    cells, place, raw_w, proj, taps, outgoing, held, part_out, part_far, part_near,
    base, hidden, strip_out, strip_in, filled, shifted, hidden1,
    cells_sem, raw_sem, taps_sem, msg_send, msg_recv,
    far_send, far_recv, near_send, near_recv, halo_send, halo_recv,
):
    sec = lax.axis_index("section")
    lat = lax.axis_index("lat")
    lon = lax.axis_index("lon")
    core = lax.rem(lat, 2)
    long_way = 1 - 2 * core

    def at_z(step):
        return lax.rem(lon + step + 2 * LON, LON)

    cells_copy = pltpu.make_async_copy(fields.at[0], cells, cells_sem)
    cells_copy.start()
    sources = (lon, at_z(-2 * long_way), at_z(-long_way), at_z(long_way))
    raw_copies = []
    for q, z in enumerate(sources):
        copy = pltpu.make_async_copy(embed_w.at[:, z], raw_w.at[q], raw_sem.at[q])
        copy.start()
        raw_copies.append(copy)
    taps_copy = pltpu.make_async_copy(conv_w, taps, taps_sem)
    taps_copy.start()

    row_tile = sec * LAT + lat
    above = lax.rem(row_tile + 31, 32)
    below = lax.rem(row_tile + 1, 32)

    def tile_device(row, z):
        return (row // LAT, lax.rem(row, LAT), z)

    west, east = at_z(-1), at_z(1)
    corners = ((above, west), (above, east), (below, west), (below, east))

    def lat_peer(s):
        x = lax.rem(lat // 4 + s // 4, 4)
        y = lax.rem(lat // 2 + s // 2, 2)
        c = lax.rem(lat + s, 2)
        return x * 4 + y * 2 + c, c

    barrier = pltpu.get_barrier_semaphore()

    def greet(device):
        pl.semaphore_signal(barrier, inc=1, device_id=device, device_id_type=MESH)

    def greet_lat(s, carry):
        peer, _ = lat_peer(s)
        greet((sec, peer, at_z(-2 * long_way)))
        greet((sec, peer, west))
        greet((sec, peer, east))

        @pl.when(s > 0)
        def _():
            greet((sec, peer, lon))

        return carry

    lax.fori_loop(0, LAT, greet_lat, 0)
    greet(tile_device(above, lon))
    greet(tile_device(below, lon))
    for row, z in corners:
        greet(tile_device(row, z))

    row_id = lax.broadcasted_iota(jnp.int32, place.shape, 0) - MAX_SHIFT
    lane_id = lax.broadcasted_iota(jnp.int32, place.shape, 1)
    wanted = (row_id % PATCH) * PITCH + 2 + row_id // PATCH
    hit = (row_id >= 0) & (row_id < CELL_COLS) & (wanted == lane_id)
    place[...] = jnp.where(hit, 1.0, 0.0).astype(BF16)

    sub = lax.broadcasted_iota(jnp.int32, (64, 8, 128), 1) // 4
    lane = lax.broadcasted_iota(jnp.int32, (64, 8, 128), 2) // 64
    keep = sub == lane

    def arrange(slot, offset):
        z = at_z(offset)
        start = jnp.minimum((z * CELL_COLS) // 128 * 128, LAST_START)
        shift = MAX_SHIFT - (z * CELL_COLS - start)
        window = cells[:, pl.ds(pl.multiple_of(start, 128), WINDOW)]
        chosen = place[pl.ds(pl.multiple_of(shift, 16), WINDOW), :]
        moved = jnp.dot(window, chosen, preferred_element_type=F32).reshape(64, 8, 256)
        halves = []
        for j in range(2):
            part = moved[:, :, j * 128 : (j + 1) * 128]
            turned = pltpu.roll(pltpu.roll(part, 4, 1), 64, 2)
            halves.append(jnp.where(keep, part, turned))
        block = jnp.concatenate(halves, axis=1).astype(BF16).reshape(LAT, 4, 16, 128)
        for i in range(4):
            outgoing[slot, :, :, i * 128 : (i + 1) * 128] = block[:, i]

    def send_step(t):
        reach = (2, 1, -1, 0, 0, 0, 0, 0)[t]

        def send(s, carry):
            peer, c = lat_peer(s)
            way = 1 - 2 * c
            slot = t if t in (0, 7) else (t + c if t % 2 else t - c)
            pltpu.make_async_remote_copy(
                src_ref=outgoing.at[slot, peer],
                dst_ref=held.at[t, lat],
                send_sem=msg_send.at[t],
                recv_sem=msg_recv.at[t],
                device_id=(sec, peer, at_z(reach * way)),
                device_id_type=MESH,
            ).start()
            return carry

        lax.fori_loop(0 if reach else 1, LAT, send, 0)
        if not reach:
            slot = t if t == 7 else (t + core if t % 2 else t - core)
            held[t, pl.ds(lat, 1)] = outgoing[slot, pl.ds(lat, 1)]

    def wait_step(t, sem):
        count = LAT if t < 3 else LAT - 1
        view = held.at[t, pl.ds(0, count)]
        pltpu.make_async_copy(view, view, sem.at[t]).wait()

    cells_copy.wait()
    arrange(0, 4)
    pl.semaphore_wait(barrier, 3 * LAT + LAT - 1 + 6)
    send_step(0)
    arrange(1, 3)
    arrange(2, -3)
    send_step(1)
    arrange(3, 2)
    arrange(4, -2)
    send_step(3)
    send_step(2)
    send_step(4)
    arrange(5, 1)
    arrange(6, -1)
    send_step(5)
    send_step(6)
    arrange(7, 0)
    send_step(7)

    new = lax.broadcasted_iota(jnp.int32, (BLOCK, BLOCK), 0)
    old = lax.broadcasted_iota(jnp.int32, (BLOCK, BLOCK), 1)
    source = (new // 16) * 16 + (new % 4) * 4 + (new % 16) // 4
    swap = jnp.where(source == old, 1.0, 0.0).astype(BF16)
    for q in range(4):
        raw_copies[q].wait()
        rows = raw_w[q].astype(F32).reshape(BLOCK, WIDTH).astype(BF16)
        proj[q] = jnp.dot(swap, rows, preferred_element_type=F32).astype(BF16)

    def project(t, q, c):
        block = held[t, :, :, c * CHUNK : (c + 1) * CHUNK].reshape(BLOCK, CHUNK)
        return lax.dot_general(block, proj[q], (((0,), (0,)), ((), ())), preferred_element_type=F32)

    def part_copy(stage, way, c):
        landing = (part_far, part_near)[stage]
        return pltpu.make_async_remote_copy(
            src_ref=part_out.at[stage, way, c],
            dst_ref=landing.at[way, c],
            send_sem=(far_send, near_send)[stage].at[way, c],
            recv_sem=(far_recv, near_recv)[stage].at[way, c],
            device_id=(sec, lat, at_z((1 - 2 * way) * long_way)),
            device_id_type=MESH,
        )

    wait_step(0, msg_recv)
    wait_step(1, msg_recv)
    wait_step(3, msg_recv)
    for c in ORDER:
        total = project(0, 1, c) + project(1, 2, c) + project(3, 0, c)
        part_out[0, 0, c] = total.astype(BF16)
        part_copy(0, 0, c).start()
    wait_step(2, msg_recv)
    wait_step(4, msg_recv)
    for c in ORDER:
        total = project(2, 3, c) + project(4, 0, c)
        part_out[0, 1, c] = total.astype(BF16)
        part_copy(0, 1, c).start()
    wait_step(5, msg_recv)
    wait_step(6, msg_recv)
    for c in ORDER:
        for way in range(2):
            mine = project(5 + way, 0, c)
            part_copy(0, way, c).wait_recv()
            part_out[1, way, c] = (mine + part_far[way, c].astype(F32)).astype(BF16)
            part_copy(1, way, c).start()
    wait_step(7, msg_recv)
    for c in ORDER:
        base[c] = project(7, 0, c) + embed_b[...]

    def halo_copy(k, src, dst, device):
        return pltpu.make_async_remote_copy(
            src_ref=src,
            dst_ref=dst,
            send_sem=halo_send.at[k],
            recv_sem=halo_recv.at[k],
            device_id=device,
            device_id_type=MESH,
        )

    top, bottom = hidden.at[pl.ds(0, CHUNK)], hidden.at[pl.ds(PADDED - CHUNK, CHUNK)]
    first, last = hidden.at[pl.ds(CHUNK, CHUNK)], hidden.at[pl.ds(CHUNK * CHUNKS, CHUNK)]
    to_above = halo_copy(0, first, bottom, tile_device(above, lon))
    to_below = halo_copy(1, last, top, tile_device(below, lon))
    for c in ORDER:
        total = base[c]
        for way in range(2):
            part_copy(1, way, c).wait_recv()
            total = total + part_near[way, c].astype(F32)
        hidden[pl.ds(CHUNK * (c + 1), CHUNK)] = total.astype(BF16)
        if c == 0:
            to_above.start()
        if c == CHUNKS - 1:
            to_below.start()

    own = hidden[pl.ds(CHUNK, TOKENS)]
    entry = lax.broadcasted_iota(jnp.int32, (32, TOKENS), 0)
    token = lax.broadcasted_iota(jnp.int32, (32, TOKENS), 1)
    edge = (entry % 16 // 2) * PITCH + 2 + entry % 2 + (entry // 16) * (COLS - 2)
    pick = jnp.where(edge == token, 1.0, 0.0).astype(BF16)
    strips = jnp.dot(pick, own, preferred_element_type=F32).astype(BF16)
    strip_out[...] = strips.reshape(2, 16, WIDTH)
    sends = (
        (1, (row_tile, east), 0),
        (0, (row_tile, west), 1),
        (1, (below, east), 2),
        (0, (below, west), 3),
        (1, (above, east), 4),
        (0, (above, west), 5),
    )
    strip_copies = []
    for side, (row, z), slot in sends:
        copy = halo_copy(2 + slot, strip_out.at[side], strip_in.at[slot], tile_device(row, z))
        copy.start()
        strip_copies.append(copy)

    def normalize(values):
        scale = lax.rsqrt(jnp.mean(values * values, axis=-1, keepdims=True) + EPS)
        return values * scale

    def spread(target, at, values):
        rows = values.shape[0]
        target[pl.ds(at, rows), 0:WIDTH] = pltpu.roll(values, 1, 0).astype(BF16)
        target[pl.ds(at, rows), WIDTH : 2 * WIDTH] = values.astype(BF16)
        target[pl.ds(at, rows), 2 * WIDTH : 3 * WIDTH] = pltpu.roll(values, rows - 1, 0).astype(BF16)

    def inside(at, rows):
        row = (lax.broadcasted_iota(jnp.int32, (rows, 1), 0) + at) // PITCH
        return ((row >= 2) | (row_tile > 0)) & ((row < ROWS + 2) | (row_tile < 31))

    taps_copy.wait()
    to_above.wait_recv()
    to_below.wait_recv()
    for copy in strip_copies:
        copy.wait_recv()
    received = strip_in[...].reshape(96, WIDTH)
    for at in range(0, PADDED, 256):
        spot = lax.broadcasted_iota(jnp.int32, (256, 96), 0) + at
        item = lax.broadcasted_iota(jnp.int32, (256, 96), 1)
        group, entry = item // 32, item % 16
        row = entry // 2 + jnp.where(group == 0, 2, jnp.where(group == 1, -6, ROWS + 2))
        column = entry % 2 + (item // 16 % 2) * (COLS + 2)
        fill = jnp.where((spot // PITCH == row) & (spot % PITCH == column), 1.0, 0.0).astype(BF16)
        placed = jnp.dot(fill, received, preferred_element_type=F32)
        column = lax.broadcasted_iota(jnp.int32, (256, 1), 0) % PITCH
        inner = (column >= 2) & (column < COLS + 2)
        values = jnp.where(inner, hidden[pl.ds(at, 256)].astype(F32), placed)
        values = jnp.where(inside(at, 256), values, 0.0)
        filled[pl.ds(at, 256)] = values.astype(BF16)
        spread(shifted, at, normalize(values))

    def conv(layer, at, rows):
        total = jnp.dot(shifted[pl.ds(at, rows)], taps[layer, 0], preferred_element_type=F32)
        for i in (1, 2):
            total += jnp.dot(shifted[pl.ds(at + i * PITCH, rows)], taps[layer, i], preferred_element_type=F32)
        return total + conv_b[layer : layer + 1]

    half = (ROWS + 2) * PITCH // 2
    normed = []
    for at in (0, half):
        before = filled[pl.ds(at + PITCH, half)].astype(F32)
        after = (before + jax.nn.gelu(conv(0, at, half))).astype(BF16).astype(F32)
        after = jnp.where(inside(at + PITCH, half), after, 0.0)
        hidden1[pl.ds(at, half)] = after.astype(BF16)
        normed.append(normalize(after))
    for at, values in zip((0, half), normed):
        spread(shifted, at, values)
    half = TOKENS // 2
    for at in (0, half):
        before = hidden1[pl.ds(at + PITCH, half)].astype(F32)
        after = before + jax.nn.gelu(conv(1, at, half))
        after = after.reshape(half // PITCH, PITCH, WIDTH)[:, 2 : COLS + 2]
        out[pl.ds(at // PITCH, half // PITCH)] = after.astype(BF16)

    for t in range(8):
        wait_step(t, msg_send)
    for stage in range(2):
        for way in range(2):
            for c in range(CHUNKS):
                part_copy(stage, way, c).wait_send()
    to_above.wait_send()
    to_below.wait_send()
    for copy in strip_copies:
        copy.wait_send()


def on_device(fields, embed_weight, embed_bias, conv_weights, conv_bias):
    vmem = pl.BlockSpec(memory_space=pltpu.VMEM)
    hbm = pl.BlockSpec(memory_space=pl.ANY)
    dma = pltpu.SemaphoreType.DMA
    return pl.pallas_call(
        kernel,
        out_shape=jax.ShapeDtypeStruct((ROWS, COLS, WIDTH), BF16),
        in_specs=[hbm, hbm, vmem, hbm, vmem],
        out_specs=vmem,
        scratch_shapes=[
            pltpu.VMEM((512, 1920), BF16),
            pltpu.VMEM((MAX_SHIFT + WINDOW, 256), BF16),
            pltpu.VMEM((4, LAT, PATCH, PATCH, WIDTH), BF16),
            pltpu.VMEM((4, BLOCK, WIDTH), BF16),
            pltpu.VMEM((2, 3, 3 * WIDTH, WIDTH), BF16),
            pltpu.VMEM((LON, LAT, 16, TOKENS), BF16),
            pltpu.VMEM((LON, LAT, 16, TOKENS), BF16),
            pltpu.VMEM((2, 2, CHUNKS, CHUNK, WIDTH), BF16),
            pltpu.VMEM((2, CHUNKS, CHUNK, WIDTH), BF16),
            pltpu.VMEM((2, CHUNKS, CHUNK, WIDTH), BF16),
            pltpu.VMEM((CHUNKS, CHUNK, WIDTH), F32),
            pltpu.VMEM((PADDED, WIDTH), BF16),
            pltpu.VMEM((2, 16, WIDTH), BF16),
            pltpu.VMEM((6, 16, WIDTH), BF16),
            pltpu.VMEM((PADDED, WIDTH), BF16),
            pltpu.VMEM((PADDED, 3 * WIDTH), BF16),
            pltpu.VMEM(((ROWS + 2) * PITCH, WIDTH), BF16),
            dma,
            dma((4,)),
            dma,
            dma((LON,)),
            dma((LON,)),
            dma((2, CHUNKS)),
            dma((2, CHUNKS)),
            dma((2, CHUNKS)),
            dma((2, CHUNKS)),
            dma((8,)),
            dma((8,)),
        ],
        compiler_params=pltpu.CompilerParams(
            collective_id=0, has_side_effects=True, vmem_limit_bytes=52 * 1024 * 1024
        ),
        cost_estimate=pl.CostEstimate(flops=7_000_000_000, bytes_accessed=14_000_000, transcendentals=600_000),
    )(
        fields,
        embed_weight.reshape(LAT, LON, PATCH, PATCH, WIDTH),
        embed_bias.reshape(1, WIDTH),
        conv_weights.reshape(2, 3, 3 * WIDTH, WIDTH),
        conv_bias,
    )


def solution(mesh):
    return jax.shard_map(
        on_device,
        mesh=mesh,
        in_specs=(P(("lat", "lon"), "section", None), P(), P(), P(), P()),
        out_specs=P(("section", "lat"), "lon", None),
        check_vma=False,
    )
```

```python
import jax
import jax.numpy as jnp
from jax import lax
from jax.experimental import pallas as pl
from jax.experimental.pallas import tpu as pltpu
from jax.sharding import PartitionSpec as P

MESH = pl.DeviceIdType.MESH
F32 = jnp.float32
BF16 = jnp.bfloat16

LAT = 16
LON = 8
PATCH = 4
ROWS = 8
COLS = 60
WIDTH = 512
PITCH = 64
TOKENS = ROWS * PITCH
CELL_COLS = COLS * PATCH
WINDOW = 384
SIDE = 128
NCOLS = 1920
FIRST = SIDE - 2 * PATCH
MAX_SHIFT = FIRST % 128
CHUNKS = 4
CHUNK = TOKENS // CHUNKS
ORDER = (0, 3, 1, 2)
PADDED = (ROWS + 4) * PITCH
BLOCK = 16 * 16
EPS = 1e-06


def kernel(
    fields, embed_w, embed_bias, conv_w, conv_bias, out,
    embed_b, conv_b, cells, place, raw_w, proj, taps, outgoing, held, part_out, part_far, part_near,
    base, hidden, shifted, hidden1, shifted1,
    ready, bias_sem, cells_sem, raw_sem, taps_sem, msg_send, msg_recv,
    far_send, far_recv, near_send, near_recv, halo_send, halo_recv,
):
    sec = lax.axis_index("section")
    lat = lax.axis_index("lat")
    lon = lax.axis_index("lon")
    core = lax.rem(lat, 2)
    long_way = 1 - 2 * core

    def at_z(step):
        return lax.rem(lon + step + 2 * LON, LON)

    cell_copies = []
    for k, (src, dst, size) in enumerate(((0, SIDE, NCOLS), (NCOLS - SIDE, 0, SIDE), (0, SIDE + NCOLS, SIDE))):
        copy = pltpu.make_async_copy(
            fields.at[0, :, pl.ds(src, size)], cells.at[:, pl.ds(dst, size)], cells_sem.at[k]
        )
        copy.start()
        cell_copies.append(copy)
    sources = (lon, at_z(-2 * long_way), at_z(-long_way), at_z(long_way))
    raw_copies = []
    for q, z in enumerate(sources):
        copy = pltpu.make_async_copy(embed_w.at[:, z], raw_w.at[q], raw_sem.at[q])
        copy.start()
        raw_copies.append(copy)
    bias_copies = (
        pltpu.make_async_copy(embed_bias, embed_b, bias_sem.at[0]),
        pltpu.make_async_copy(conv_bias, conv_b, bias_sem.at[1]),
    )
    for copy in bias_copies:
        copy.start()
    taps_copy = pltpu.make_async_copy(conv_w, taps, taps_sem)

    row_tile = sec * LAT + lat
    above = lax.rem(row_tile + 31, 32)
    below = lax.rem(row_tile + 1, 32)

    def tile_device(row, z):
        return (row // LAT, lax.rem(row, LAT), z)

    def lat_peer(s):
        u = lax.rem(s + 6, LAT)
        x = lax.rem(lat // 4 + 1 + 2 * u + u // 2, 4)
        y = lax.rem(lat // 2 + u, 2)
        c = lax.rem(lat + u // 8, 2)
        return x * 4 + y * 2 + c, c

    barrier = pltpu.get_barrier_semaphore()
    planes = tuple((sec, lat, at_z(step)) for step in (1, -1, 2, -2))
    row_peers = (tile_device(above, lon), tile_device(below, lon))

    def greet(semaphore, device):
        pl.semaphore_signal(semaphore, inc=1, device_id=device, device_id_type=MESH)

    for device in planes + row_peers:
        greet(barrier, device)

    def greet_lat(s, carry):
        peer, _ = lat_peer(s)
        greet(barrier, (sec, peer, lon))
        return carry

    lax.fori_loop(1, LAT, greet_lat, 0)

    row_id = lax.broadcasted_iota(jnp.int32, place.shape, 0) - MAX_SHIFT
    lane_id = lax.broadcasted_iota(jnp.int32, place.shape, 1)
    wanted = (row_id % PATCH) * PITCH + row_id // PATCH
    hit = (row_id >= 0) & (row_id < PITCH * PATCH) & (wanted == lane_id)
    place[...] = jnp.where(hit, 1.0, 0.0).astype(BF16)

    sub = lax.broadcasted_iota(jnp.int32, (64, 8, 128), 1) // 4
    lane = lax.broadcasted_iota(jnp.int32, (64, 8, 128), 2) // 64
    keep = sub == lane

    def arrange(slot, offset):
        z = at_z(offset)
        begin = z * CELL_COLS + FIRST
        start = begin // 128 * 128
        shift = MAX_SHIFT - (begin - start)
        window = cells[:, pl.ds(pl.multiple_of(start, 128), WINDOW)]
        chosen = place[pl.ds(pl.multiple_of(shift, 16), WINDOW), :]
        moved = jnp.dot(window, chosen, preferred_element_type=F32).reshape(64, 8, 256)
        halves = []
        for j in range(2):
            part = moved[:, :, j * 128 : (j + 1) * 128]
            turned = pltpu.roll(pltpu.roll(part, 4, 1), 64, 2)
            halves.append(jnp.where(keep, part, turned))
        block = jnp.concatenate(halves, axis=1).astype(BF16).reshape(LAT, 4, 16, 128)
        for i in range(4):
            outgoing[slot, :, :, i * 128 : (i + 1) * 128] = block[:, i]

    def slot_of(t, c):
        return t if t in (0, 7) else (t + c if t % 2 else t - c)

    def send_one(t, s):
        peer, c = lat_peer(s)
        reach = (2, 1, -1, 0, 0, 0, 0, 0)[t]
        pltpu.make_async_remote_copy(
            src_ref=outgoing.at[slot_of(t, c), peer],
            dst_ref=held.at[t, lat],
            send_sem=msg_send.at[t],
            recv_sem=msg_recv.at[t],
            device_id=(sec, peer, at_z(reach * (1 - 2 * c))),
            device_id_type=MESH,
        ).start()

    def send_steps(steps, first, last):
        def send(s, carry):
            for t in steps:
                send_one(t, s)
            return carry

        lax.fori_loop(first, last, send, 0)

    def wait_step(t, sem):
        count = LAT if t < 3 else LAT - 1
        view = held.at[t, pl.ds(0, count)]
        pltpu.make_async_copy(view, view, sem.at[t]).wait()

    for copy in cell_copies:
        copy.wait()
    for slot, offset in enumerate((4, 3, -3, 2, -2, 1, -1, 0)):
        arrange(slot, offset)

    new = lax.broadcasted_iota(jnp.int32, (BLOCK, BLOCK), 0)
    old = lax.broadcasted_iota(jnp.int32, (BLOCK, BLOCK), 1)
    source = (new // 16) * 16 + (new % 4) * 4 + (new % 16) // 4
    swap = jnp.where(source == old, 1.0, 0.0).astype(BF16)
    for q in range(4):
        raw_copies[q].wait()
        rows = raw_w[q].astype(F32).reshape(BLOCK, WIDTH).astype(BF16)
        proj[q] = jnp.dot(swap, rows, preferred_element_type=F32).astype(BF16)

    for copy in bias_copies:
        copy.wait()
    taps_copy.start()

    pl.semaphore_wait(barrier, LAT - 1 + 6)
    for device in planes:
        greet(ready, device)
    send_steps((3,), 1, 8)
    pl.semaphore_wait(ready, 4)
    send_steps((0, 1), 0, 8)
    send_steps((0, 1, 3), 8, LAT)
    send_steps((2,), 0, 1)
    send_steps((2, 4), 1, LAT)
    send_steps((5, 6), 1, LAT)
    send_steps((7,), 1, LAT)
    for t in range(3, 8):
        held[t, pl.ds(lat, 1)] = outgoing[slot_of(t, core), pl.ds(lat, 1)]

    def project(t, q, c):
        block = held[t, :, :, c * CHUNK : (c + 1) * CHUNK].reshape(BLOCK, CHUNK)
        return lax.dot_general(block, proj[q], (((0,), (0,)), ((), ())), preferred_element_type=F32)

    def part_copy(stage, way, c):
        landing = (part_far, part_near)[stage]
        return pltpu.make_async_remote_copy(
            src_ref=part_out.at[stage, way, c],
            dst_ref=landing.at[way, c],
            send_sem=(far_send, near_send)[stage].at[way, c],
            recv_sem=(far_recv, near_recv)[stage].at[way, c],
            device_id=(sec, lat, at_z((1 - 2 * way) * long_way)),
            device_id_type=MESH,
        )

    wait_step(0, msg_recv)
    wait_step(1, msg_recv)
    wait_step(3, msg_recv)
    for c in ORDER:
        total = project(0, 1, c) + project(1, 2, c) + project(3, 0, c)
        part_out[0, 0, c] = total.astype(BF16)
        part_copy(0, 0, c).start()
    wait_step(2, msg_recv)
    wait_step(4, msg_recv)
    for c in ORDER:
        total = project(2, 3, c) + project(4, 0, c)
        part_out[0, 1, c] = total.astype(BF16)
        part_copy(0, 1, c).start()
    wait_step(5, msg_recv)
    wait_step(6, msg_recv)
    for c in ORDER:
        for way in range(2):
            mine = project(5 + way, 0, c)
            part_copy(0, way, c).wait_recv()
            part_out[1, way, c] = (mine + part_far[way, c].astype(F32)).astype(BF16)
            part_copy(1, way, c).start()
    wait_step(7, msg_recv)
    for c in ORDER:
        base[c] = project(7, 0, c) + embed_b[...]

    def halo_copy(k, src, dst, device):
        return pltpu.make_async_remote_copy(
            src_ref=src,
            dst_ref=dst,
            send_sem=halo_send.at[k],
            recv_sem=halo_recv.at[k],
            device_id=device,
            device_id_type=MESH,
        )

    top, bottom = hidden.at[pl.ds(0, CHUNK)], hidden.at[pl.ds(PADDED - CHUNK, CHUNK)]
    first, last = hidden.at[pl.ds(CHUNK, CHUNK)], hidden.at[pl.ds(CHUNK * CHUNKS, CHUNK)]
    to_above = halo_copy(0, first, bottom, tile_device(above, lon))
    to_below = halo_copy(1, last, top, tile_device(below, lon))

    def normalize(values):
        scale = lax.rsqrt(jnp.mean(values * values, axis=-1, keepdims=True) + EPS)
        return values * scale

    def spread(target, at, values):
        rows = values.shape[0]
        target[pl.ds(at, rows), 0:WIDTH] = pltpu.roll(values, 1, 0).astype(BF16)
        target[pl.ds(at, rows), WIDTH : 2 * WIDTH] = values.astype(BF16)
        target[pl.ds(at, rows), 2 * WIDTH : 3 * WIDTH] = pltpu.roll(values, rows - 1, 0).astype(BF16)

    def inside(at, rows):
        row = (lax.broadcasted_iota(jnp.int32, (rows, 1), 0) + at) // PITCH
        return ((row >= 2) | (row_tile > 0)) & ((row < ROWS + 2) | (row_tile < 31))

    def finish_tokens(c):
        total = base[c]
        for way in range(2):
            part_copy(1, way, c).wait_recv()
            total = total + part_near[way, c].astype(F32)
        tokens = total.astype(BF16)
        at = CHUNK * (c + 1)
        hidden[pl.ds(at, CHUNK)] = tokens
        if c == 0:
            to_above.start()
        if c == CHUNKS - 1:
            to_below.start()
        spread(shifted, at, normalize(tokens.astype(F32)))

    def take_halo(copy, at):
        copy.wait_recv()
        values = jnp.where(inside(at, CHUNK), hidden[pl.ds(at, CHUNK)].astype(F32), 0.0)
        spread(shifted, at, normalize(values))

    def conv(source, layer, at, rows):
        total = jnp.dot(source[pl.ds(at, rows)], taps[layer, 0], preferred_element_type=F32)
        for i in (1, 2):
            total += jnp.dot(source[pl.ds(at + i * PITCH, rows)], taps[layer, i], preferred_element_type=F32)
        return total + conv_b[layer : layer + 1]

    def first_layer(row, count):
        at, rows = row * PITCH, count * PITCH
        before = hidden[pl.ds(at, rows)].astype(F32)
        after = (before + jax.nn.gelu(conv(shifted, 0, at - PITCH, rows))).astype(BF16).astype(F32)
        if row < 2 or row + count > ROWS + 2:
            after = jnp.where(inside(at, rows), after, 0.0)
        hidden1[pl.ds(at, rows)] = after.astype(BF16)
        spread(shifted1, at, normalize(after))

    def second_layer(row, count):
        at, rows = row * PITCH, count * PITCH
        before = hidden1[pl.ds(at, rows)].astype(F32)
        after = before + jax.nn.gelu(conv(shifted1, 1, at - PITCH, rows))
        after = after.reshape(count, PITCH, WIDTH)[:, 2 : COLS + 2]
        out[pl.ds(row - 2, count)] = after.astype(BF16)

    finish_tokens(0)
    finish_tokens(3)
    finish_tokens(1)
    taps_copy.wait()
    take_halo(to_below, 0)
    take_halo(to_above, PADDED - CHUNK)
    first_layer(1, 4)
    first_layer(9, 2)
    second_layer(2, 2)
    finish_tokens(2)
    first_layer(5, 4)
    second_layer(4, 6)

    for t in range(8):
        wait_step(t, msg_send)
    for stage in range(2):
        for way in range(2):
            for c in range(CHUNKS):
                part_copy(stage, way, c).wait_send()
    to_above.wait_send()
    to_below.wait_send()


def on_device(fields, embed_weight, embed_bias, conv_weights, conv_bias):
    vmem = pl.BlockSpec(memory_space=pltpu.VMEM)
    hbm = pl.BlockSpec(memory_space=pl.ANY)
    dma = pltpu.SemaphoreType.DMA
    return pl.pallas_call(
        kernel,
        out_shape=jax.ShapeDtypeStruct((ROWS, COLS, WIDTH), BF16),
        in_specs=[hbm] * 5,
        out_specs=vmem,
        scratch_shapes=[
            pltpu.VMEM((1, WIDTH), F32),
            pltpu.VMEM((2, WIDTH), F32),
            pltpu.VMEM((512, NCOLS + 2 * SIDE), BF16),
            pltpu.VMEM((512, 256), BF16),
            pltpu.VMEM((4, LAT, PATCH, PATCH, WIDTH), BF16),
            pltpu.VMEM((4, BLOCK, WIDTH), BF16),
            pltpu.VMEM((2, 3, 3 * WIDTH, WIDTH), BF16),
            pltpu.VMEM((LON, LAT, 16, TOKENS), BF16),
            pltpu.VMEM((LON, LAT, 16, TOKENS), BF16),
            pltpu.VMEM((2, 2, CHUNKS, CHUNK, WIDTH), BF16),
            pltpu.VMEM((2, CHUNKS, CHUNK, WIDTH), BF16),
            pltpu.VMEM((2, CHUNKS, CHUNK, WIDTH), BF16),
            pltpu.VMEM((CHUNKS, CHUNK, WIDTH), F32),
            pltpu.VMEM((PADDED, WIDTH), BF16),
            pltpu.VMEM((PADDED, 3 * WIDTH), BF16),
            pltpu.VMEM((PADDED, WIDTH), BF16),
            pltpu.VMEM((PADDED, 3 * WIDTH), BF16),
            pltpu.SemaphoreType.REGULAR,
            dma((2,)),
            dma((3,)),
            dma((4,)),
            dma,
            dma((LON,)),
            dma((LON,)),
            dma((2, CHUNKS)),
            dma((2, CHUNKS)),
            dma((2, CHUNKS)),
            dma((2, CHUNKS)),
            dma((2,)),
            dma((2,)),
        ],
        compiler_params=pltpu.CompilerParams(
            collective_id=0, has_side_effects=True, vmem_limit_bytes=52 * 1024 * 1024
        ),
        cost_estimate=pl.CostEstimate(flops=7_000_000_000, bytes_accessed=14_000_000, transcendentals=600_000),
    )(
        fields,
        embed_weight.reshape(LAT, LON, PATCH, PATCH, WIDTH),
        embed_bias.reshape(1, WIDTH),
        conv_weights.reshape(2, 3, 3 * WIDTH, WIDTH),
        conv_bias,
    )


def solution(mesh):
    return jax.shard_map(
        on_device,
        mesh=mesh,
        in_specs=(P(("lat", "lon"), "section", None), P(), P(), P(), P()),
        out_specs=P(("section", "lat"), "lon", None),
        check_vma=False,
    )
```

```python
import jax
import jax.numpy as jnp
from jax import lax
from jax.experimental import pallas as pl
from jax.experimental.pallas import tpu as pltpu
from jax.sharding import PartitionSpec as P

MESH = pl.DeviceIdType.MESH
F32 = jnp.float32
BF16 = jnp.bfloat16

LAT = 16
LON = 8
PATCH = 4
ROWS = 8
COLS = 60
WIDTH = 512
PITCH = 64
TOKENS = ROWS * PITCH
CELL_COLS = COLS * PATCH
WINDOW = 384
SIDE = 128
NCOLS = 1920
FIRST = SIDE - 2 * PATCH
MAX_SHIFT = FIRST % 128
CHUNKS = 4
CHUNK = TOKENS // CHUNKS
PADDED = (ROWS + 4) * PITCH
BLOCK = 16 * 16
EPS = 1e-06


def kernel(
    fields, embed_w, embed_bias, conv_w, conv_bias, out,
    embed_b, conv_b, cells, place, raw_w, proj, taps, outgoing, held, part_out, part_far, part_near,
    base, hidden, shifted, hidden1, shifted1,
    ready, bias_sem, cells_sem, raw_sem, taps_sem, msg_send, msg_recv,
    far_send, far_recv, near_send, near_recv, halo_send, halo_recv,
):
    sec = lax.axis_index("section")
    lat = lax.axis_index("lat")
    lon = lax.axis_index("lon")
    core = lax.rem(lat, 2)
    long_way = 1 - 2 * core

    def at_z(step):
        return lax.rem(lon + step + 2 * LON, LON)

    cell_copies = []
    for k, (src, dst, size) in enumerate(((0, SIDE, NCOLS), (NCOLS - SIDE, 0, SIDE), (0, SIDE + NCOLS, SIDE))):
        copy = pltpu.make_async_copy(
            fields.at[0, :, pl.ds(src, size)], cells.at[:, pl.ds(dst, size)], cells_sem.at[k]
        )
        copy.start()
        cell_copies.append(copy)
    sources = (lon, at_z(-2 * long_way), at_z(-long_way), at_z(long_way))
    raw_copies = []
    for q, z in enumerate(sources):
        copy = pltpu.make_async_copy(embed_w.at[:, z], raw_w.at[q], raw_sem.at[q])
        copy.start()
        raw_copies.append(copy)
    bias_copies = (
        pltpu.make_async_copy(embed_bias, embed_b, bias_sem.at[0]),
        pltpu.make_async_copy(conv_bias, conv_b, bias_sem.at[1]),
    )
    for copy in bias_copies:
        copy.start()
    taps_copy = pltpu.make_async_copy(conv_w, taps, taps_sem)

    row_tile = sec * LAT + lat
    above = lax.rem(row_tile + 31, 32)
    below = lax.rem(row_tile + 1, 32)

    def tile_device(row, z):
        return (row // LAT, lax.rem(row, LAT), z)

    def lat_peer(s):
        u = lax.rem(s + 6, LAT)
        x = lax.rem(lat // 4 + 1 + 2 * u + u // 2, 4)
        y = lax.rem(lat // 2 + u, 2)
        c = lax.rem(lat + u // 8, 2)
        return x * 4 + y * 2 + c, c

    barrier = pltpu.get_barrier_semaphore()
    planes = tuple((sec, lat, at_z(step)) for step in (1, -1, 2, -2))
    row_peers = (tile_device(above, lon), tile_device(below, lon))

    def greet(semaphore, device):
        pl.semaphore_signal(semaphore, inc=1, device_id=device, device_id_type=MESH)

    for device in planes + row_peers:
        greet(barrier, device)

    def greet_lat(s, carry):
        peer, _ = lat_peer(s)
        greet(barrier, (sec, peer, lon))
        return carry

    lax.fori_loop(1, LAT, greet_lat, 0)

    row_id = lax.broadcasted_iota(jnp.int32, place.shape, 0) - MAX_SHIFT
    lane_id = lax.broadcasted_iota(jnp.int32, place.shape, 1)
    wanted = (row_id % PATCH) * PITCH + row_id // PATCH
    hit = (row_id >= 0) & (row_id < PITCH * PATCH) & (wanted == lane_id)
    place[...] = jnp.where(hit, 1.0, 0.0).astype(BF16)

    sub = lax.broadcasted_iota(jnp.int32, (64, 8, 128), 1) // 4
    lane = lax.broadcasted_iota(jnp.int32, (64, 8, 128), 2) // 64
    keep = sub == lane

    def arrange(slot, offset):
        z = at_z(offset)
        begin = z * CELL_COLS + FIRST
        start = begin // 128 * 128
        shift = MAX_SHIFT - (begin - start)
        window = cells[:, pl.ds(pl.multiple_of(start, 128), WINDOW)]
        chosen = place[pl.ds(pl.multiple_of(shift, 16), WINDOW), :]
        moved = jnp.dot(window, chosen, preferred_element_type=F32).reshape(64, 8, 256)
        halves = []
        for j in range(2):
            part = moved[:, :, j * 128 : (j + 1) * 128]
            turned = pltpu.roll(pltpu.roll(part, 4, 1), 64, 2)
            halves.append(jnp.where(keep, part, turned))
        block = jnp.concatenate(halves, axis=1).astype(BF16).reshape(LAT, 4, 16, 128)
        for i in range(4):
            outgoing[slot, :, :, i * 128 : (i + 1) * 128] = block[:, i]

    def slot_of(t, c):
        return t if t in (0, 7) else (t + c if t % 2 else t - c)

    def send_one(t, s):
        peer, c = lat_peer(s)
        reach = (2, 1, -1, 0, 0, 0, 0, 0)[t]
        pltpu.make_async_remote_copy(
            src_ref=outgoing.at[slot_of(t, c), peer],
            dst_ref=held.at[t, lat],
            send_sem=msg_send.at[t],
            recv_sem=msg_recv.at[t],
            device_id=(sec, peer, at_z(reach * (1 - 2 * c))),
            device_id_type=MESH,
        ).start()

    def send_steps(steps, first, last):
        def send(s, carry):
            for t in steps:
                send_one(t, s)
            return carry

        lax.fori_loop(first, last, send, 0)

    def wait_step(t, sem):
        count = LAT if t < 3 else LAT - 1
        view = held.at[t, pl.ds(0, count)]
        pltpu.make_async_copy(view, view, sem.at[t]).wait()

    for copy in cell_copies:
        copy.wait()
    for slot, offset in enumerate((4, 3, -3, 2, -2, 1, -1, 0)):
        arrange(slot, offset)

    new = lax.broadcasted_iota(jnp.int32, (BLOCK, BLOCK), 0)
    old = lax.broadcasted_iota(jnp.int32, (BLOCK, BLOCK), 1)
    source = (new // 16) * 16 + (new % 4) * 4 + (new % 16) // 4
    swap = jnp.where(source == old, 1.0, 0.0).astype(BF16)
    for q in range(4):
        raw_copies[q].wait()
        rows = raw_w[q].astype(F32).reshape(BLOCK, WIDTH).astype(BF16)
        proj[q] = jnp.dot(swap, rows, preferred_element_type=F32).astype(BF16)

    for copy in bias_copies:
        copy.wait()
    taps_copy.start()

    pl.semaphore_wait(barrier, LAT - 1 + 6)
    for device in planes:
        greet(ready, device)
    send_steps((3,), 1, 8)
    pl.semaphore_wait(ready, 4)
    send_steps((0, 1), 0, 8)
    send_steps((0, 1, 3), 8, LAT)
    send_steps((2,), 0, 1)
    send_steps((2, 4), 1, LAT)
    send_steps((5, 6), 1, LAT)
    send_steps((7,), 1, LAT)
    for t in range(3, 8):
        held[t, pl.ds(lat, 1)] = outgoing[slot_of(t, core), pl.ds(lat, 1)]

    def project(t, q, c):
        block = held[t, :, :, c * CHUNK : (c + 1) * CHUNK].reshape(BLOCK, CHUNK)
        return lax.dot_general(block, proj[q], (((0,), (0,)), ((), ())), preferred_element_type=F32)

    def part_copy(stage, way, c):
        landing = (part_far, part_near)[stage]
        return pltpu.make_async_remote_copy(
            src_ref=part_out.at[stage, way, c],
            dst_ref=landing.at[way, c],
            send_sem=(far_send, near_send)[stage].at[way, c],
            recv_sem=(far_recv, near_recv)[stage].at[way, c],
            device_id=(sec, lat, at_z((1 - 2 * way) * long_way)),
            device_id_type=MESH,
        )

    def send_far(way, c):
        if way == 0:
            total = project(0, 1, c) + project(1, 2, c) + project(3, 0, c)
        else:
            total = project(2, 3, c) + project(4, 0, c)
        part_out[0, way, c] = total.astype(BF16)
        part_copy(0, way, c).start()

    def send_near(c):
        for way in range(2):
            mine = project(5 + way, 0, c)
            part_copy(0, way, c).wait_recv()
            part_out[1, way, c] = (mine + part_far[way, c].astype(F32)).astype(BF16)
            part_copy(1, way, c).start()

    for t in (0, 1, 3):
        wait_step(t, msg_recv)
    for c in (0, 3, 1):
        send_far(0, c)
    for t in (2, 4):
        wait_step(t, msg_recv)
    for c in (0, 3, 1):
        send_far(1, c)
    for t in (5, 6):
        wait_step(t, msg_recv)
    send_near(0)
    send_near(3)
    for way in range(2):
        send_far(way, 2)
    wait_step(7, msg_recv)
    for c in range(CHUNKS):
        base[c] = project(7, 0, c) + embed_b[...]
    send_near(1)

    def halo_copy(k, src, dst, device):
        return pltpu.make_async_remote_copy(
            src_ref=src,
            dst_ref=dst,
            send_sem=halo_send.at[k],
            recv_sem=halo_recv.at[k],
            device_id=device,
            device_id_type=MESH,
        )

    top, bottom = hidden.at[pl.ds(0, CHUNK)], hidden.at[pl.ds(PADDED - CHUNK, CHUNK)]
    first, last = hidden.at[pl.ds(CHUNK, CHUNK)], hidden.at[pl.ds(CHUNK * CHUNKS, CHUNK)]
    to_above = halo_copy(0, first, bottom, tile_device(above, lon))
    to_below = halo_copy(1, last, top, tile_device(below, lon))

    def normalize(values):
        scale = lax.rsqrt(jnp.mean(values * values, axis=-1, keepdims=True) + EPS)
        return values * scale

    def spread(target, at, values):
        rows = values.shape[0]
        target[pl.ds(at, rows), 0:WIDTH] = pltpu.roll(values, 1, 0).astype(BF16)
        target[pl.ds(at, rows), WIDTH : 2 * WIDTH] = values.astype(BF16)
        target[pl.ds(at, rows), 2 * WIDTH : 3 * WIDTH] = pltpu.roll(values, rows - 1, 0).astype(BF16)

    def inside(at, rows):
        row = (lax.broadcasted_iota(jnp.int32, (rows, 1), 0) + at) // PITCH
        return ((row >= 2) | (row_tile > 0)) & ((row < ROWS + 2) | (row_tile < 31))

    def finish_tokens(c):
        total = base[c]
        for way in range(2):
            part_copy(1, way, c).wait_recv()
            total = total + part_near[way, c].astype(F32)
        tokens = total.astype(BF16)
        at = CHUNK * (c + 1)
        hidden[pl.ds(at, CHUNK)] = tokens
        if c == 0:
            to_above.start()
        if c == CHUNKS - 1:
            to_below.start()
        spread(shifted, at, normalize(tokens.astype(F32)))

    def take_halo(copy, at):
        copy.wait_recv()
        values = jnp.where(inside(at, CHUNK), hidden[pl.ds(at, CHUNK)].astype(F32), 0.0)
        spread(shifted, at, normalize(values))

    def conv(source, layer, at, rows):
        total = jnp.dot(source[pl.ds(at, rows)], taps[layer, 0], preferred_element_type=F32)
        for i in (1, 2):
            total += jnp.dot(source[pl.ds(at + i * PITCH, rows)], taps[layer, i], preferred_element_type=F32)
        return total + conv_b[layer : layer + 1]

    def first_layer(row, count):
        at, rows = row * PITCH, count * PITCH
        before = hidden[pl.ds(at, rows)].astype(F32)
        after = (before + jax.nn.gelu(conv(shifted, 0, at - PITCH, rows))).astype(BF16).astype(F32)
        if row < 2 or row + count > ROWS + 2:
            after = jnp.where(inside(at, rows), after, 0.0)
        hidden1[pl.ds(at, rows)] = after.astype(BF16)
        spread(shifted1, at, normalize(after))

    def second_layer(row, count):
        at, rows = row * PITCH, count * PITCH
        before = hidden1[pl.ds(at, rows)].astype(F32)
        after = before + jax.nn.gelu(conv(shifted1, 1, at - PITCH, rows))
        after = after.reshape(count, PITCH, WIDTH)[:, 2 : COLS + 2]
        out[pl.ds(row - 2, count)] = after.astype(BF16)

    finish_tokens(0)
    finish_tokens(3)
    send_near(2)
    taps_copy.wait()
    take_halo(to_below, 0)
    first_layer(1, 2)
    take_halo(to_above, PADDED - CHUNK)
    first_layer(9, 2)
    finish_tokens(1)
    first_layer(3, 2)
    second_layer(2, 2)
    finish_tokens(2)
    first_layer(5, 2)
    first_layer(7, 2)
    second_layer(4, 3)
    second_layer(7, 3)

    for t in range(8):
        wait_step(t, msg_send)
    for stage in range(2):
        for way in range(2):
            for c in range(CHUNKS):
                part_copy(stage, way, c).wait_send()
    to_above.wait_send()
    to_below.wait_send()


def on_device(fields, embed_weight, embed_bias, conv_weights, conv_bias):
    vmem = pl.BlockSpec(memory_space=pltpu.VMEM)
    hbm = pl.BlockSpec(memory_space=pl.ANY)
    dma = pltpu.SemaphoreType.DMA
    return pl.pallas_call(
        kernel,
        out_shape=jax.ShapeDtypeStruct((ROWS, COLS, WIDTH), BF16),
        in_specs=[hbm] * 5,
        out_specs=vmem,
        scratch_shapes=[
            pltpu.VMEM((1, WIDTH), F32),
            pltpu.VMEM((2, WIDTH), F32),
            pltpu.VMEM((512, NCOLS + 2 * SIDE), BF16),
            pltpu.VMEM((512, 256), BF16),
            pltpu.VMEM((4, LAT, PATCH, PATCH, WIDTH), BF16),
            pltpu.VMEM((4, BLOCK, WIDTH), BF16),
            pltpu.VMEM((2, 3, 3 * WIDTH, WIDTH), BF16),
            pltpu.VMEM((LON, LAT, 16, TOKENS), BF16),
            pltpu.VMEM((LON, LAT, 16, TOKENS), BF16),
            pltpu.VMEM((2, 2, CHUNKS, CHUNK, WIDTH), BF16),
            pltpu.VMEM((2, CHUNKS, CHUNK, WIDTH), BF16),
            pltpu.VMEM((2, CHUNKS, CHUNK, WIDTH), BF16),
            pltpu.VMEM((CHUNKS, CHUNK, WIDTH), F32),
            pltpu.VMEM((PADDED, WIDTH), BF16),
            pltpu.VMEM((PADDED, 3 * WIDTH), BF16),
            pltpu.VMEM((PADDED, WIDTH), BF16),
            pltpu.VMEM((PADDED, 3 * WIDTH), BF16),
            pltpu.SemaphoreType.REGULAR,
            dma((2,)),
            dma((3,)),
            dma((4,)),
            dma,
            dma((LON,)),
            dma((LON,)),
            dma((2, CHUNKS)),
            dma((2, CHUNKS)),
            dma((2, CHUNKS)),
            dma((2, CHUNKS)),
            dma((2,)),
            dma((2,)),
        ],
        compiler_params=pltpu.CompilerParams(
            collective_id=0, has_side_effects=True, vmem_limit_bytes=52 * 1024 * 1024
        ),
        cost_estimate=pl.CostEstimate(flops=7_000_000_000, bytes_accessed=14_000_000, transcendentals=600_000),
    )(
        fields,
        embed_weight.reshape(LAT, LON, PATCH, PATCH, WIDTH),
        embed_bias.reshape(1, WIDTH),
        conv_weights.reshape(2, 3, 3 * WIDTH, WIDTH),
        conv_bias,
    )


def solution(mesh):
    return jax.shard_map(
        on_device,
        mesh=mesh,
        in_specs=(P(("lat", "lon"), "section", None), P(), P(), P(), P()),
        out_specs=P(("section", "lat"), "lon", None),
        check_vma=False,
    )
```

```python
import jax
import jax.numpy as jnp
from jax import lax
from jax.experimental import pallas as pl
from jax.experimental.pallas import tpu as pltpu
from jax.sharding import PartitionSpec as P

MESH = pl.DeviceIdType.MESH
F32 = jnp.float32
BF16 = jnp.bfloat16

LAT = 16
LON = 8
PATCH = 4
ROWS = 8
COLS = 60
WIDTH = 512
PITCH = 64
TOKENS = ROWS * PITCH
CELL_COLS = COLS * PATCH
WINDOW = 384
SIDE = 128
NCOLS = 1920
FIRST = SIDE - 2 * PATCH
MAX_SHIFT = FIRST % 128
CHUNKS = 4
CHUNK = TOKENS // CHUNKS
PADDED = (ROWS + 4) * PITCH
BLOCK = 16 * 16
EPS = 1e-06


def kernel(
    fields, embed_w, embed_bias, conv_w, conv_bias, out,
    embed_b, conv_b, cells, place, raw_w, proj, taps, outgoing, held, part_out, part_far, part_near,
    base, hidden, shifted, hidden1, shifted1,
    ready, bias_sem, cells_sem, raw_sem, taps_sem, msg_send, msg_recv,
    far_send, far_recv, near_send, near_recv, halo_send, halo_recv,
):
    sec = lax.axis_index("section")
    lat = lax.axis_index("lat")
    lon = lax.axis_index("lon")
    core = lax.rem(lat, 2)
    long_way = 1 - 2 * core

    def at_z(step):
        return lax.rem(lon + step + 2 * LON, LON)

    cell_copies = []
    for k, (src, dst, size) in enumerate(((0, SIDE, NCOLS), (NCOLS - SIDE, 0, SIDE), (0, SIDE + NCOLS, SIDE))):
        copy = pltpu.make_async_copy(
            fields.at[0, :, pl.ds(src, size)], cells.at[:, pl.ds(dst, size)], cells_sem.at[k]
        )
        copy.start()
        cell_copies.append(copy)
    sources = (lon, at_z(-2 * long_way), at_z(-long_way), at_z(long_way))
    raw_copies = []
    for q, z in enumerate(sources):
        copy = pltpu.make_async_copy(embed_w.at[:, z], raw_w.at[q], raw_sem.at[q])
        copy.start()
        raw_copies.append(copy)
    bias_copies = (
        pltpu.make_async_copy(embed_bias, embed_b, bias_sem.at[0]),
        pltpu.make_async_copy(conv_bias, conv_b, bias_sem.at[1]),
    )
    for copy in bias_copies:
        copy.start()
    taps_copy = pltpu.make_async_copy(conv_w, taps, taps_sem)

    row_tile = sec * LAT + lat
    above = lax.rem(row_tile + 31, 32)
    below = lax.rem(row_tile + 1, 32)

    def tile_device(row, z):
        return (row // LAT, lax.rem(row, LAT), z)

    def lat_peer(s):
        u = lax.rem(s + 6, LAT)
        x = lax.rem(lat // 4 + 1 + 2 * u + u // 2, 4)
        y = lax.rem(lat // 2 + u, 2)
        c = lax.rem(lat + u // 8, 2)
        return x * 4 + y * 2 + c, c

    barrier = pltpu.get_barrier_semaphore()
    planes = tuple((sec, lat, at_z(step)) for step in (1, -1, 2, -2))
    row_peers = (tile_device(above, lon), tile_device(below, lon))

    def greet(semaphore, device):
        pl.semaphore_signal(semaphore, inc=1, device_id=device, device_id_type=MESH)

    for device in planes + row_peers:
        greet(barrier, device)

    def greet_lat(s, carry):
        peer, _ = lat_peer(s)
        greet(barrier, (sec, peer, lon))
        return carry

    lax.fori_loop(1, LAT, greet_lat, 0)

    row_id = lax.broadcasted_iota(jnp.int32, place.shape, 0) - MAX_SHIFT
    lane_id = lax.broadcasted_iota(jnp.int32, place.shape, 1)
    wanted = (row_id % PATCH) * PITCH + row_id // PATCH
    hit = (row_id >= 0) & (row_id < PITCH * PATCH) & (wanted == lane_id)
    place[...] = jnp.where(hit, 1.0, 0.0).astype(BF16)

    sub = lax.broadcasted_iota(jnp.int32, (64, 8, 128), 1) // 4
    lane = lax.broadcasted_iota(jnp.int32, (64, 8, 128), 2) // 64
    keep = sub == lane

    def arrange(slot, offset):
        z = at_z(offset)
        begin = z * CELL_COLS + FIRST
        start = begin // 128 * 128
        shift = MAX_SHIFT - (begin - start)
        window = cells[:, pl.ds(pl.multiple_of(start, 128), WINDOW)]
        chosen = place[pl.ds(pl.multiple_of(shift, 16), WINDOW), :]
        moved = jnp.dot(window, chosen, preferred_element_type=F32).reshape(64, 8, 256)
        halves = []
        for j in range(2):
            part = moved[:, :, j * 128 : (j + 1) * 128]
            turned = pltpu.roll(pltpu.roll(part, 4, 1), 64, 2)
            halves.append(jnp.where(keep, part, turned))
        block = jnp.concatenate(halves, axis=1).astype(BF16).reshape(LAT, 4, 16, 128)
        for i in range(4):
            outgoing[slot, :, :, i * 128 : (i + 1) * 128] = block[:, i]

    def slot_of(t, c):
        return t if t in (0, 7) else (t + c if t % 2 else t - c)

    def send_one(t, s):
        peer, c = lat_peer(s)
        reach = (2, 1, -1, 0, 0, 0, 0, 0)[t]
        pltpu.make_async_remote_copy(
            src_ref=outgoing.at[slot_of(t, c), peer],
            dst_ref=held.at[t, lat],
            send_sem=msg_send.at[t],
            recv_sem=msg_recv.at[t],
            device_id=(sec, peer, at_z(reach * (1 - 2 * c))),
            device_id_type=MESH,
        ).start()

    def send_steps(steps, first, last):
        def send(s, carry):
            for t in steps:
                send_one(t, s)
            return carry

        lax.fori_loop(first, last, send, 0)

    def wait_step(t, sem):
        count = LAT if t < 3 else LAT - 1
        view = held.at[t, pl.ds(0, count)]
        pltpu.make_async_copy(view, view, sem.at[t]).wait()

    for copy in cell_copies:
        copy.wait()
    for slot, offset in enumerate((4, 3, -3, 2, -2, 1, -1, 0)):
        arrange(slot, offset)

    new = lax.broadcasted_iota(jnp.int32, (BLOCK, BLOCK), 0)
    old = lax.broadcasted_iota(jnp.int32, (BLOCK, BLOCK), 1)
    source = (new // 16) * 16 + (new % 4) * 4 + (new % 16) // 4
    swap = jnp.where(source == old, 1.0, 0.0).astype(BF16)
    for q in range(4):
        raw_copies[q].wait()
        rows = raw_w[q].astype(F32).reshape(BLOCK, WIDTH).astype(BF16)
        proj[q] = jnp.dot(swap, rows, preferred_element_type=F32).astype(BF16)

    for copy in bias_copies:
        copy.wait()
    taps_copy.start()

    pl.semaphore_wait(barrier, LAT - 1 + 6)
    for device in planes:
        greet(ready, device)
    send_steps((3,), 1, LAT)
    pl.semaphore_wait(ready, 4)
    send_steps((0, 1), 0, LAT)
    send_steps((2,), 0, 1)
    send_steps((2, 4), 1, LAT)
    send_steps((5, 6), 1, LAT)
    send_steps((7,), 1, LAT)
    for t in range(3, 8):
        held[t, pl.ds(lat, 1)] = outgoing[slot_of(t, core), pl.ds(lat, 1)]

    def project(t, q, c):
        block = held[t, :, :, c * CHUNK : (c + 1) * CHUNK].reshape(BLOCK, CHUNK)
        return lax.dot_general(block, proj[q], (((0,), (0,)), ((), ())), preferred_element_type=F32)

    def part_copy(stage, way, c):
        landing = (part_far, part_near)[stage]
        return pltpu.make_async_remote_copy(
            src_ref=part_out.at[stage, way, c],
            dst_ref=landing.at[way, c],
            send_sem=(far_send, near_send)[stage].at[way, c],
            recv_sem=(far_recv, near_recv)[stage].at[way, c],
            device_id=(sec, lat, at_z((1 - 2 * way) * long_way)),
            device_id_type=MESH,
        )

    def send_far(way, c):
        if way == 0:
            total = project(0, 1, c) + project(1, 2, c) + project(3, 0, c)
        else:
            total = project(2, 3, c) + project(4, 0, c)
        part_out[0, way, c] = total.astype(BF16)
        part_copy(0, way, c).start()

    def send_near(c):
        for way in range(2):
            mine = project(5 + way, 0, c)
            part_copy(0, way, c).wait_recv()
            part_out[1, way, c] = (mine + part_far[way, c].astype(F32)).astype(BF16)
            part_copy(1, way, c).start()

    for t in (0, 1, 3):
        wait_step(t, msg_recv)
    for c in (0, 3, 1):
        send_far(0, c)
    for t in (2, 4):
        wait_step(t, msg_recv)
    for c in (0, 3, 1):
        send_far(1, c)
    for t in (5, 6):
        wait_step(t, msg_recv)
    send_near(0)
    send_near(3)
    for way in range(2):
        send_far(way, 2)
    wait_step(7, msg_recv)
    for c in range(CHUNKS):
        base[c] = project(7, 0, c) + embed_b[...]
    send_near(1)

    def halo_copy(k, src, dst, device):
        return pltpu.make_async_remote_copy(
            src_ref=src,
            dst_ref=dst,
            send_sem=halo_send.at[k],
            recv_sem=halo_recv.at[k],
            device_id=device,
            device_id_type=MESH,
        )

    top, bottom = hidden.at[pl.ds(0, CHUNK)], hidden.at[pl.ds(PADDED - CHUNK, CHUNK)]
    first, last = hidden.at[pl.ds(CHUNK, CHUNK)], hidden.at[pl.ds(CHUNK * CHUNKS, CHUNK)]
    to_above = halo_copy(0, first, bottom, tile_device(above, lon))
    to_below = halo_copy(1, last, top, tile_device(below, lon))

    def normalize(values):
        scale = lax.rsqrt(jnp.mean(values * values, axis=-1, keepdims=True) + EPS)
        return values * scale

    def spread(target, at, values):
        rows = values.shape[0]
        target[pl.ds(at, rows), 0:WIDTH] = pltpu.roll(values, 1, 0).astype(BF16)
        target[pl.ds(at, rows), WIDTH : 2 * WIDTH] = values.astype(BF16)
        target[pl.ds(at, rows), 2 * WIDTH : 3 * WIDTH] = pltpu.roll(values, rows - 1, 0).astype(BF16)

    def inside(at, rows):
        row = (lax.broadcasted_iota(jnp.int32, (rows, 1), 0) + at) // PITCH
        return ((row >= 2) | (row_tile > 0)) & ((row < ROWS + 2) | (row_tile < 31))

    def finish_tokens(c):
        total = base[c]
        for way in range(2):
            part_copy(1, way, c).wait_recv()
            total = total + part_near[way, c].astype(F32)
        tokens = total.astype(BF16)
        at = CHUNK * (c + 1)
        hidden[pl.ds(at, CHUNK)] = tokens
        if c == 0:
            to_above.start()
        if c == CHUNKS - 1:
            to_below.start()
        spread(shifted, at, normalize(tokens.astype(F32)))

    def take_halo(copy, at):
        copy.wait_recv()
        values = jnp.where(inside(at, CHUNK), hidden[pl.ds(at, CHUNK)].astype(F32), 0.0)
        spread(shifted, at, normalize(values))

    def conv(source, layer, at, rows):
        total = jnp.dot(source[pl.ds(at, rows)], taps[layer, 0], preferred_element_type=F32)
        for i in (1, 2):
            total += jnp.dot(source[pl.ds(at + i * PITCH, rows)], taps[layer, i], preferred_element_type=F32)
        return total + conv_b[layer : layer + 1]

    def first_layer(row, count):
        at, rows = row * PITCH, count * PITCH
        before = hidden[pl.ds(at, rows)].astype(F32)
        after = (before + jax.nn.gelu(conv(shifted, 0, at - PITCH, rows))).astype(BF16).astype(F32)
        if row < 2 or row + count > ROWS + 2:
            after = jnp.where(inside(at, rows), after, 0.0)
        hidden1[pl.ds(at, rows)] = after.astype(BF16)
        spread(shifted1, at, normalize(after))

    def second_layer(row, count):
        at, rows = row * PITCH, count * PITCH
        before = hidden1[pl.ds(at, rows)].astype(F32)
        after = before + jax.nn.gelu(conv(shifted1, 1, at - PITCH, rows))
        after = after.reshape(count, PITCH, WIDTH)[:, 2 : COLS + 2]
        out[pl.ds(row - 2, count)] = after.astype(BF16)

    finish_tokens(0)
    finish_tokens(3)
    send_near(2)
    taps_copy.wait()
    take_halo(to_below, 0)
    first_layer(1, 2)
    take_halo(to_above, PADDED - CHUNK)
    first_layer(9, 2)
    finish_tokens(1)
    first_layer(3, 2)
    second_layer(2, 2)
    finish_tokens(2)
    first_layer(5, 2)
    first_layer(7, 2)
    second_layer(4, 3)
    second_layer(7, 3)

    for t in range(8):
        wait_step(t, msg_send)
    for stage in range(2):
        for way in range(2):
            for c in range(CHUNKS):
                part_copy(stage, way, c).wait_send()
    to_above.wait_send()
    to_below.wait_send()


def on_device(fields, embed_weight, embed_bias, conv_weights, conv_bias):
    vmem = pl.BlockSpec(memory_space=pltpu.VMEM)
    hbm = pl.BlockSpec(memory_space=pl.ANY)
    dma = pltpu.SemaphoreType.DMA
    return pl.pallas_call(
        kernel,
        out_shape=jax.ShapeDtypeStruct((ROWS, COLS, WIDTH), BF16),
        in_specs=[hbm] * 5,
        out_specs=vmem,
        scratch_shapes=[
            pltpu.VMEM((1, WIDTH), F32),
            pltpu.VMEM((2, WIDTH), F32),
            pltpu.VMEM((512, NCOLS + 2 * SIDE), BF16),
            pltpu.VMEM((512, 256), BF16),
            pltpu.VMEM((4, LAT, PATCH, PATCH, WIDTH), BF16),
            pltpu.VMEM((4, BLOCK, WIDTH), BF16),
            pltpu.VMEM((2, 3, 3 * WIDTH, WIDTH), BF16),
            pltpu.VMEM((LON, LAT, 16, TOKENS), BF16),
            pltpu.VMEM((LON, LAT, 16, TOKENS), BF16),
            pltpu.VMEM((2, 2, CHUNKS, CHUNK, WIDTH), BF16),
            pltpu.VMEM((2, CHUNKS, CHUNK, WIDTH), BF16),
            pltpu.VMEM((2, CHUNKS, CHUNK, WIDTH), BF16),
            pltpu.VMEM((CHUNKS, CHUNK, WIDTH), F32),
            pltpu.VMEM((PADDED, WIDTH), BF16),
            pltpu.VMEM((PADDED, 3 * WIDTH), BF16),
            pltpu.VMEM((PADDED, WIDTH), BF16),
            pltpu.VMEM((PADDED, 3 * WIDTH), BF16),
            pltpu.SemaphoreType.REGULAR,
            dma((2,)),
            dma((3,)),
            dma((4,)),
            dma,
            dma((LON,)),
            dma((LON,)),
            dma((2, CHUNKS)),
            dma((2, CHUNKS)),
            dma((2, CHUNKS)),
            dma((2, CHUNKS)),
            dma((2,)),
            dma((2,)),
        ],
        compiler_params=pltpu.CompilerParams(
            collective_id=0, has_side_effects=True, vmem_limit_bytes=52 * 1024 * 1024
        ),
        cost_estimate=pl.CostEstimate(flops=7_000_000_000, bytes_accessed=14_000_000, transcendentals=600_000),
    )(
        fields,
        embed_weight.reshape(LAT, LON, PATCH, PATCH, WIDTH),
        embed_bias.reshape(1, WIDTH),
        conv_weights.reshape(2, 3, 3 * WIDTH, WIDTH),
        conv_bias,
    )


def solution(mesh):
    return jax.shard_map(
        on_device,
        mesh=mesh,
        in_specs=(P(("lat", "lon"), "section", None), P(), P(), P(), P()),
        out_specs=P(("section", "lat"), "lon", None),
        check_vma=False,
    )
```
